512 devices in a mesh: row: 16 (over x, y), col: 32 (over z, core).
Axes of the slice: x: 4, y: 4, z: 16, core: 2. Of those that a mesh axis runs over, the one named last changes fastest.
Arguments:
- blocks: float32 [16, 32, 64, 128, 128], P('row', 'col')
- block_rows: int32 [16, 32, 64], P('row', 'col'), may hold values from 0 to 31
- block_cols: int32 [16, 32, 64], P('row', 'col'), may hold values from 0 to 15
- block_valid: int32 [16, 32, 64], P('row', 'col'), may hold values from 0 to 1, as said below
- rhs: float32 [16, 32, 64, 128], P('row', 'col')
Outputs:
- solution: float32 [16, 32, 64, 128], P('row', 'col')
The draws below stay inside these ranges and needn't reach their ends.
Inputs may be any that keep to these rules, and one draw needn't show every extreme that they name: `block_valid`: in each device's list the valid slots come first; every device has at least 16 valid slots, and at least one device has all 64 slots valid.
All inputs are finite; a program needn't handle non-finite values.
Results may differ from the reference program's by a relative error of at most 0.0003.
Values sent between devices are 32-bit elements; how exact they have to be, the bound alone decides.
No kernel may reach another device: no remote copies, remote signals or barrier semaphores. Data moves between devices by JAX's collectives and lax.ppermute only.
A program may use at most 64 MiB of HBM per device.

```python
import math
import jax
import jax.numpy as jnp
from jax import lax

BLK = 128
RBL = 32
CBL = 16
NB = 64
NRHS = 64
ITERS = 2
N_ROW = 16
N_COL = 32


def draw_blocks(key, part):
    key = jax.random.fold_in(key, 11)
    first, second = jax.random.split(key)
    shape = (N_ROW, N_COL, NB, BLK, BLK)
    spread = jnp.exp(jax.random.uniform(second, shape, jnp.float32) * math.log(10.0))
    rising = 1.0 + 2.0 * jnp.arange(N_COL, dtype=jnp.float32) / max(N_COL - 1, 1)
    factor = 1.0 / (4.6 * math.sqrt(0.6 * NB * N_COL * BLK / RBL))
    base = jax.random.normal(first, shape, jnp.float32)
    return base * spread * rising[None, :, None, None, None] * factor


def draw_rhs(key, part):
    key = jax.random.fold_in(key, 23)
    first, second = jax.random.split(key)
    piece_len = RBL * BLK // N_COL
    shape = (N_ROW, N_COL, NRHS, piece_len)
    spread = jnp.exp(jax.random.uniform(second, shape, jnp.float32) * math.log(10.0))
    grow = jnp.arange(N_ROW, dtype=jnp.float32)[:, None, None, None] * (RBL * BLK) + jnp.arange(N_COL, dtype=jnp.float32)[None, :, None, None] * piece_len + jnp.arange(piece_len, dtype=jnp.float32)[None, None, None, :]
    rising = 1.0 + 2.0 * grow / (N_ROW * RBL * BLK - 1)
    base = jax.random.normal(first, shape, jnp.float32)
    return base * spread * rising * 0.3


def draw_block_valid(key, part):
    key = jax.random.fold_in(key, 37)
    first, second = jax.random.split(key)
    counts = jax.random.randint(first, (N_ROW, N_COL), NB // 4, NB + 1)
    chosen = jax.random.randint(second, (), 0, N_ROW * N_COL)
    flat = jnp.arange(N_ROW * N_COL, dtype=jnp.int32).reshape(N_ROW, N_COL)
    counts = jnp.where(flat == chosen, NB, counts)
    slots = jnp.arange(NB, dtype=jnp.int32)
    return (slots[None, None, :] < counts[:, :, None]).astype(jnp.int32)


def touch_ends(entries, stream_key, smallest, high):
    longest = entries.shape.index(max(entries.shape))
    spots = []
    for shift in (0, 1):
        where = [jax.random.randint(jax.random.fold_in(stream_key, axis), (), 0, length) for axis, length in enumerate(entries.shape)]
        where[longest] = (where[longest] + shift) % entries.shape[longest]
        spots.append(tuple(where))
    return entries.at[spots[0]].set(smallest).at[spots[1]].set(high)


def setup_inputs(seed: int = 0) -> dict:
    key_of = jax.random.split(jax.random.key(seed), 6)
    blocks = draw_blocks(jax.random.fold_in(key_of[5], 71), 0)
    block_rows = touch_ends(jax.random.randint(key_of[1], (N_ROW, N_COL, NB), 0, RBL), jax.random.fold_in(key_of[1], 1), 0, RBL - 1).astype(jnp.int32)
    block_cols = touch_ends(jax.random.randint(key_of[2], (N_ROW, N_COL, NB), 0, CBL), jax.random.fold_in(key_of[2], 1), 0, CBL - 1).astype(jnp.int32)
    block_valid = draw_block_valid(jax.random.fold_in(key_of[5], 71), 0)
    rhs = draw_rhs(jax.random.fold_in(key_of[5], 71), 0)
    return dict(blocks=blocks, block_rows=block_rows, block_cols=block_cols, block_valid=block_valid, rhs=rhs)


HIGH = lax.Precision.HIGHEST
eps = 1e-06

def reference(blocks, block_rows, block_cols, block_valid, rhs):
    count = NRHS
    valid = block_valid.astype(jnp.float32)
    col_base = (jnp.arange(N_COL, dtype=jnp.int32) * CBL)[:, None]
    row_range = jnp.arange(RBL, dtype=jnp.int32)

    def forward(vec):
        tiles_all = vec.reshape(count, N_COL * CBL, BLK)

        def one_row(index):
            gidx = (col_base + block_cols[index]).reshape(-1).astype(jnp.int32)
            tiles = jnp.take(tiles_all, gidx, axis=1)
            mats = blocks[index].reshape(N_COL * NB, BLK, BLK)
            prod = jnp.einsum('sab,ksb->ksa', mats, tiles, precision=HIGH)
            onehot = (block_rows[index].reshape(-1)[:, None] == row_range[None, :]).astype(jnp.float32)
            onehot = onehot * valid[index].reshape(-1)[:, None]
            return jnp.einsum('sr,ksa->kra', onehot, prod, precision=HIGH).reshape(count, RBL * BLK)
        result = lax.map(one_row, jnp.arange(N_ROW, dtype=jnp.int32))
        return result.transpose(1, 0, 2).reshape(count, N_ROW * RBL * BLK)

    def backward(vec):
        tiles_all = vec.reshape(count, N_ROW, RBL, BLK)

        def step(total, index):
            urow = lax.dynamic_index_in_dim(tiles_all, index, 1, keepdims=False)
            tiles = jnp.take(urow, block_rows[index].reshape(-1).astype(jnp.int32), axis=1)
            mats = blocks[index].reshape(N_COL * NB, BLK, BLK)
            prod = jnp.einsum('sab,ksa->ksb', mats, tiles, precision=HIGH)
            prod = prod * valid[index].reshape(-1)[None, :, None]
            gidx = (col_base + block_cols[index]).reshape(-1).astype(jnp.int32)
            contrib = jax.ops.segment_sum(prod.transpose(1, 0, 2), gidx, num_segments=N_COL * CBL)
            return (total + contrib, None)
        start = jnp.zeros((N_COL * CBL, count, BLK), jnp.float32)
        total, _ = lax.scan(step, start, jnp.arange(N_ROW, dtype=jnp.int32))
        return total.transpose(1, 0, 2).reshape(count, N_COL * CBL * BLK)

    def norm(vec):
        return jnp.sqrt(lax.optimization_barrier(jnp.sum(vec * vec, axis=1)) + eps)
    data = rhs.transpose(2, 0, 1, 3).reshape(count, N_ROW * RBL * BLK)
    beta = norm(data)
    u_vec = data / beta[:, None]
    v_vec = backward(u_vec)
    alpha = norm(v_vec)
    v_vec = v_vec / alpha[:, None]
    w_vec = v_vec
    x_vec = jnp.zeros_like(v_vec)
    phibar = beta
    rhobar = alpha
    for step_index in range(ITERS):
        u_vec = forward(v_vec) - alpha[:, None] * u_vec
        beta = norm(u_vec)
        u_vec = u_vec / beta[:, None]
        v_vec = backward(u_vec) - beta[:, None] * v_vec
        alpha = norm(v_vec)
        v_vec = v_vec / alpha[:, None]
        rho = jnp.sqrt(rhobar * rhobar + beta * beta)
        cosine = rhobar / rho
        sine = beta / rho
        theta = sine * alpha
        rhobar = -cosine * alpha
        phi = cosine * phibar
        phibar = sine * phibar
        x_vec = x_vec + (phi / rho)[:, None] * w_vec
        w_vec = v_vec - (theta / rho)[:, None] * w_vec
    vp_len = CBL * BLK // N_ROW
    return x_vec.reshape(count, N_COL, N_ROW, vp_len).transpose(2, 1, 0, 3)
```

```python
import jax
import jax.numpy as jnp
from jax import lax
from jax.experimental import pallas as pl
from jax.experimental.pallas import tpu as pltpu
from jax.sharding import Mesh, PartitionSpec as P

W = 128
SLOTS = 64
RBL = 32
CBL = 16
NZ = 16
ITERS = 2
PAD = 8
eps = 1e-06
SCALE = 0.25

F32 = jnp.float32
BF16 = jnp.bfloat16
NT = (((1,), (1,)), ((), ()))

SMEM = pl.BlockSpec(memory_space=pltpu.SMEM)
VMEM = pl.BlockSpec(memory_space=pltpu.VMEM)
PARAMS = pltpu.CompilerParams(vmem_limit_bytes=32 << 20)


def root(total):
    return jnp.sqrt(total + eps)


def halves(x):
    hi = x.astype(BF16)
    return hi, (x - hi.astype(F32)).astype(BF16)


def diagonal(count):
    shape = (count, W)
    return lax.broadcasted_iota(jnp.int32, shape, 0) == lax.broadcasted_iota(jnp.int32, shape, 1)


def to_row(col):
    return jnp.sum(jnp.where(diagonal(col.shape[0]), col, 0.0), axis=0, keepdims=True)


def to_col(row, count):
    return jnp.sum(jnp.where(diagonal(count), row, 0.0), axis=1, keepdims=True)


def spread(col):
    return jnp.broadcast_to(col, (col.shape[0], W))


def norm_rows(squares):
    return jnp.broadcast_to(to_row(jnp.sum(squares, axis=1, keepdims=True)), (PAD, W))


def backward_kernel(rows, cols, valid, core, mats, own, other, out, parts, acc):
    me = core[0]
    count = own.shape[1]
    squares = jnp.zeros((count, W), F32)
    for z in range(NZ):
        for ref, c in ((own, me), (other, 1 - me)):
            x = ref[z]
            squares += x * x
            parts[2 * z + c] = jnp.concatenate(halves(x * SCALE), axis=1)
    acc[...] = jnp.zeros_like(acc)
    for s in range(SLOTS):
        target = jnp.where(valid[s] > 0, cols[s], CBL)
        hi, lo = halves(mats[s])
        u = parts[rows[s]]
        prod = jnp.dot(u, jnp.concatenate([hi, hi], axis=0), preferred_element_type=F32)
        prod += jnp.dot(u[:, :W], lo, preferred_element_type=F32)
        acc[target] += prod
    out[:, :count, :] = acc[:CBL]
    out[:, count:, :] = jnp.broadcast_to(norm_rows(squares)[None], (CBL, PAD, W))


def forward_kernel(rows, cols, valid, core, mats, vec, mine, theirs, parts, acc):
    me = core[0]
    count = vec.shape[1]
    squares = jnp.zeros((count, W), F32)
    for c in range(CBL):
        x = vec[c]
        squares += x * x
        parts[c] = jnp.concatenate(halves(x * SCALE), axis=1)
    acc[...] = jnp.zeros_like(acc)
    for s in range(SLOTS):
        target = jnp.where(valid[s] > 0, rows[s], RBL)
        hi, lo = halves(mats[s])
        v = parts[cols[s]]
        prod = lax.dot_general(v, jnp.concatenate([hi, hi], axis=1), NT, preferred_element_type=F32)
        prod += lax.dot_general(v[:, :W], lo, NT, preferred_element_type=F32)
        acc[target] += prod
    norms = norm_rows(squares)
    for z in range(NZ):
        mine[z, :count] = acc[2 * z + me]
        theirs[z, :count] = acc[2 * z + 1 - me]
        mine[z, count:] = norms
        theirs[z, count:] = norms


def gathered(got, count):
    total = got[0]
    for index in range(1, got.shape[0]):
        total += got[index]
    return total[:count], root(to_col(total[count : count + 1], count))


def first_cols_kernel(got, copies, fresh, scale):
    count = fresh.shape[0]
    total, beta = gathered(got, count)
    vec = total / (SCALE * beta)
    fresh[...] = vec
    copies[...] = jnp.broadcast_to(vec[None], copies.shape)
    scale[...] = spread(beta)


def cols_kernel(got, old, alpha, copies, fresh, scale):
    count = fresh.shape[0]
    total, beta = gathered(got, count)
    vec = total / (SCALE * beta) - beta * (old[...] / alpha[...])
    fresh[...] = vec
    copies[...] = jnp.broadcast_to(vec[None], copies.shape)
    scale[...] = spread(beta)


def rows_kernel(got, old, beta, fresh, scale, norms):
    count = fresh.shape[0]
    total, alpha = gathered(got, count)
    vec = total / (SCALE * alpha) - alpha * (old[...] / beta[...])
    fresh[...] = vec
    scale[...] = spread(alpha)
    norms[...] = norm_rows(vec * vec)


def total_kernel(got, scale):
    count = scale.shape[0]
    total = got[0]
    for index in range(1, got.shape[0]):
        total += got[index]
    scale[...] = spread(root(to_col(total[:1], count)))


def call(kernel, name, specs, outs, scratch=()):
    return pl.pallas_call(
        kernel,
        out_shape=outs,
        in_specs=specs,
        out_specs=jax.tree.map(lambda _: VMEM, outs),
        scratch_shapes=scratch,
        compiler_params=PARAMS,
        name=name,
    )


def array(*shape):
    return jax.ShapeDtypeStruct(shape, F32)


def advance(state, vec, alpha, beta):
    x_vec, w_vec, phibar, rhobar = state
    rho = jnp.sqrt(rhobar * rhobar + beta * beta)
    cosine = rhobar / rho
    sine = beta / rho
    theta = sine * alpha
    rhobar = -cosine * alpha
    phi = cosine * phibar
    phibar = sine * phibar
    x_vec = x_vec + (phi / rho) * w_vec
    w_vec = vec - (theta / rho) * w_vec
    return (x_vec, w_vec, phibar, rhobar)


def on_device(blocks, block_rows, block_cols, block_valid, rhs):
    mats = blocks[0, 0]
    piece = rhs[0, 0]
    count = piece.shape[0]
    core = lax.axis_index("core").astype(jnp.int32).reshape(1)
    slots = (block_rows[0, 0], block_cols[0, 0], block_valid[0, 0], core, mats)
    swap = [(0, 1), (1, 0)]
    tile, wide = array(count, W), array(NZ, count + PAD, W)
    copied = array(CBL, count, W)

    def exchange(x, axis):
        return lax.all_to_all(x, axis, 0, 0, tiled=True)

    def backward(u_piece):
        own = lax.all_gather(u_piece, "z")
        other = lax.ppermute(own, "core", swap)
        scratch = (pltpu.VMEM((RBL, count, 2 * W), BF16), pltpu.VMEM((CBL + 1, count, W), F32))
        specs = [SMEM] * 4 + [VMEM] * 3
        part = call(backward_kernel, "apply_transposed", specs, wide, scratch)(*slots, own, other)
        return exchange(part, "row")

    def forward(copies):
        vec = exchange(copies, "row")
        scratch = (pltpu.VMEM((CBL, count, 2 * W), BF16), pltpu.VMEM((RBL + 1, count, W), F32))
        specs = [SMEM] * 4 + [VMEM] * 2
        mine, theirs = call(forward_kernel, "apply_plain", specs, (wide, wide), scratch)(*slots, vec)
        return exchange(mine + lax.ppermute(theirs, "core", swap), "z")

    def everywhere(norms):
        norms = lax.psum(norms, "core")
        for axis, length in (("z", NZ), ("row", 16)):
            norms = exchange(jnp.broadcast_to(norms[None], (length, PAD, W)), axis)
            if axis == "z":
                norms = jnp.sum(norms, axis=0)
        return call(total_kernel, "total", [VMEM], tile)(norms)

    u_old = piece
    got = backward(u_old)
    copies, v_old, beta = call(first_cols_kernel, "first_cols", [VMEM], (copied, tile, tile))(got)
    state = None
    for step_index in range(ITERS):
        got = forward(copies)
        outs = (tile, tile, array(PAD, W))
        u_old, alpha, norms = call(rows_kernel, "rows", [VMEM] * 3, outs)(got, u_old, beta)
        v_now = v_old / alpha
        if state is None:
            state = (jnp.zeros_like(v_now), v_now, beta, alpha)
        else:
            state = advance(state, v_now, alpha, beta)
        got = backward(u_old)
        copies, v_old, beta = call(cols_kernel, "cols", [VMEM] * 3, (copied, tile, tile))(got, v_old, alpha)
    beta = everywhere(norms)
    squares = jnp.sum(v_old * v_old, axis=1)
    alpha = everywhere(jnp.broadcast_to(jnp.pad(squares, (0, W - count)), (PAD, W)))
    x_out = advance(state, v_old / alpha, alpha, beta)[0]
    return x_out[None, None]


def solution(mesh):
    grid = Mesh(mesh.devices.reshape(16, NZ, 2), ("row", "z", "core"))
    col = ("z", "core")
    placed = (
        P("row", col, None, None, None),
        P("row", col, None),
        P("row", col, None),
        P("row", col, None),
        P("row", col, None, None),
    )
    return jax.shard_map(
        on_device,
        mesh=grid,
        in_specs=placed,
        out_specs=P("row", col, None, None),
        check_vma=False,
    )
```

```python
import jax
import jax.numpy as jnp
from jax import lax
from jax.experimental import pallas as pl
from jax.experimental.pallas import tpu as pltpu
from jax.sharding import Mesh, PartitionSpec as P

W = 128
SLOTS = 64
UNROLL = 32
GROUP = 16
HALF = 32
RBL = 32
CBL = 16
NZ = 16
ROWS = 16
ITERS = 2
PAD = 8
eps = 1e-06
SCALE = 0.25
TINY = 2.0**-64
LARGE = 1e37

F32 = jnp.float32
BF16 = jnp.bfloat16

SMEM = pl.BlockSpec(memory_space=pltpu.SMEM)
VMEM = pl.BlockSpec(memory_space=pltpu.VMEM)
ANY = pl.BlockSpec(memory_space=pl.ANY)
PARAMS = pltpu.CompilerParams(vmem_limit_bytes=36 << 20)


def root(total):
    return jnp.sqrt(total + eps)


def halves(x):
    hi = x.astype(BF16)
    return hi, (x - hi.astype(F32)).astype(BF16)


def diagonal(count):
    shape = (count, W)
    return lax.broadcasted_iota(jnp.int32, shape, 0) == lax.broadcasted_iota(jnp.int32, shape, 1)


def to_row(col):
    return jnp.sum(jnp.where(diagonal(col.shape[0]), col, 0.0), axis=0, keepdims=True)


def to_col(row, count):
    return jnp.sum(jnp.where(diagonal(count), row, 0.0), axis=1, keepdims=True)


def spread(col):
    return jnp.broadcast_to(col, (col.shape[0], W))


def per_vector(squares):
    total = jnp.sum(squares, axis=1, keepdims=True)
    total = total[:HALF] + total[HALF:]
    return jnp.concatenate([total, total], axis=0)


def norm_rows(squares):
    return jnp.broadcast_to(to_row(per_vector(squares)), (PAD, W))


def add_product(slots, s, side, high, low, parts, acc, source, target, unused):
    vec = parts[source(side, slots, s)]
    prod = jnp.dot(vec, jnp.concatenate([high, high], axis=0), preferred_element_type=F32)
    prod += jnp.dot(vec[:, :W], low, preferred_element_type=F32)
    acc[jnp.where(slots[2, s] > 0, target(side, slots, s), unused)] += prod


def products(sides, parts, acc, source, target, unused):
    acc[...] = jnp.zeros_like(acc)
    for side, (slots, hi, lo) in enumerate(sides):

        def group(index, carry):
            for offset in range(UNROLL):
                s = index * UNROLL + offset
                add_product(slots, s, side, hi[s], lo[s], parts, acc, source, target, unused)
            return carry

        lax.fori_loop(0, SLOTS // UNROLL, group, 0)


def by_row(side, slots, s):
    return slots[0, s]


def by_col(side, slots, s):
    return slots[1, s] + side * CBL


def store_tiles(parts, first, second, x):
    both = jnp.concatenate(halves(x * SCALE), axis=1)
    parts[first] = both[:HALF]
    parts[second] = both[HALF:]


def emit_cols(out, acc, squares):
    norms = norm_rows(squares)
    for c in range(CBL):
        out[c, :HALF] = acc[c]
        out[c, HALF : 2 * HALF] = acc[CBL + c]
        out[c, 2 * HALF :] = norms


def first_backward_kernel(slots0, slots1, mats0, mats1, vec, out, *rest):
    kept, (blocks, arrived, parts, acc) = rest[:8], rest[8:]
    groups = SLOTS // GROUP
    copies = []
    for side, mats in enumerate((mats0, mats1)):
        for index in range(groups):
            some = pl.ds(index * GROUP, GROUP)
            where = side * groups + index
            copies.append(pltpu.make_async_copy(mats.at[some], blocks.at[side, some], arrived.at[where]))
    for copy in copies:
        copy.start()
    squares = jnp.zeros((2 * HALF, W), F32)
    for z in range(NZ):
        x = vec[z]
        squares += x * x
        store_tiles(parts, 2 * z, 2 * z + 1, x)
    acc[...] = jnp.zeros_like(acc)
    for side, slots in enumerate((slots0, slots1)):
        hi, lo, hi_t, lo_t = kept[4 * side : 4 * side + 4]
        for index in range(groups):
            copies[side * groups + index].wait()
            for s in range(index * GROUP, (index + 1) * GROUP):
                block = blocks[side, s]
                high, low = halves(block)
                hi[s], lo[s] = high, low
                hi_t[s], lo_t[s] = halves(block.T)
                add_product(slots, s, side, high, low, parts, acc, by_row, by_col, 2 * CBL)
    emit_cols(out, acc, squares)


def backward_kernel(slots0, slots1, hi0, lo0, hi1, lo1, vec, out, scale, factor, parts, acc):
    count = 2 * HALF
    total = jnp.zeros((PAD, W), F32)
    for z in range(NZ):
        total += vec[z, count:]
    alpha = root(to_col(total[:1], count))
    scale[...] = spread(alpha)
    inverse = spread(1.0 / (SCALE * alpha))
    factor[...] = inverse
    squares = jnp.zeros((count, W), F32)
    for z in range(NZ):
        x = vec[z, :count] * inverse
        squares += x * x
        store_tiles(parts, 2 * z, 2 * z + 1, x)
    sides = ((slots0, hi0, lo0), (slots1, hi1, lo1))
    products(sides, parts, acc, by_row, by_col, 2 * CBL)
    emit_cols(out, acc, squares)


def forward_kernel(slots0, slots1, hi0, lo0, hi1, lo1, vec, old, first, second, out, norms, parts, acc):
    count = 2 * HALF
    squares = jnp.zeros((count, W), F32)
    for c in range(CBL):
        x = vec[c]
        squares += x * x
        store_tiles(parts, c, CBL + c, x)
    sides = ((slots0, hi0, lo0), (slots1, hi1, lo1))
    products(sides, parts, acc, by_col, by_row, RBL)
    norms[...] = norm_rows(squares)
    weight = SCALE * spread(per_vector(squares))
    for z in range(NZ):
        less = weight * ((old[z, :count] * first[...]) * second[...])
        out[z, :HALF] = acc[2 * z] - less[:HALF]
        out[z, HALF:] = acc[2 * z + 1] - less[HALF:]


def summed(got):
    total = got[0]
    for index in range(1, got.shape[0]):
        total += got[index]
    return total


def first_cols_kernel(got, copies, fresh, scale, inverse):
    count = fresh.shape[0]
    total = summed(got)
    beta = root(to_col(total[count : count + 1], count))
    vec = total[:count] / (SCALE * beta)
    fresh[...] = vec
    copies[...] = jnp.broadcast_to(vec[None], copies.shape)
    scale[...] = spread(beta)
    inverse[...] = spread(1.0 / beta)


def cols_kernel(got, old, alpha, copies, fresh, scale, inverse):
    count = fresh.shape[0]
    total = summed(got)
    beta = root(to_col(total[count : count + 1], count))
    vec = total[:count] / (SCALE * beta) - beta * (old[...] / alpha[...])
    fresh[...] = vec
    copies[...] = jnp.broadcast_to(vec[None], copies.shape)
    scale[...] = spread(beta)
    inverse[...] = spread(1.0 / beta)


def rows_kernel(got, old, first, second, norms, fresh):
    count = first.shape[0]
    fresh[:count] = summed(got) - (SCALE * eps) * ((old[:count] * first[...]) * second[...])
    fresh[count:] = norms[...]


def lanes(start):
    shape = (2 * HALF, W)
    vector = lax.rem(lax.broadcasted_iota(jnp.int32, shape, 0), HALF)
    return lax.broadcasted_iota(jnp.int32, shape, 1) == vector + start


def row_at(squares, start):
    return jnp.sum(jnp.where(lanes(start), jnp.sum(squares, axis=1, keepdims=True), 0.0), axis=0, keepdims=True)


def col_at(row, start):
    return jnp.sum(jnp.where(lanes(start), row, 0.0), axis=1, keepdims=True)


def squares_kernel(piece, out):
    count = 2 * HALF
    vec = piece[:count]
    small = vec * TINY
    norms = col_at(piece[count : count + 1], 0) * (0.5 / ROWS)
    norms = jnp.sum(jnp.where(lanes(2 * HALF), norms, 0.0), axis=0, keepdims=True)
    out[...] = row_at(vec * vec, 0) + row_at(small * small, HALF) + norms


def last_kernel(got, scale_alpha, scale_beta):
    total = got[...]
    alpha = root(col_at(total, 2 * HALF))
    plain, small = col_at(total, 0), col_at(total, HALF)
    norm = jnp.where(plain < LARGE, jnp.sqrt(plain), jnp.sqrt(small) / TINY)
    norm = norm / (SCALE * alpha)
    scale_alpha[...] = spread(alpha)
    scale_beta[...] = spread(root(norm * norm))


def total_kernel(got, scale):
    scale[...] = spread(root(col_at(got[...], 0)))


def call(kernel, name, specs, outs, scratch=()):
    return pl.pallas_call(
        kernel,
        out_shape=outs,
        in_specs=specs,
        out_specs=jax.tree.map(lambda _: VMEM, outs),
        scratch_shapes=scratch,
        compiler_params=PARAMS,
        name=name,
    )


def array(*shape):
    return jax.ShapeDtypeStruct(shape, F32)


def advance(state, vec, alpha, beta):
    x_vec, w_vec, phibar, rhobar = state
    rho = jnp.sqrt(rhobar * rhobar + beta * beta)
    cosine = rhobar / rho
    sine = beta / rho
    theta = sine * alpha
    rhobar = -cosine * alpha
    phi = cosine * phibar
    phibar = sine * phibar
    x_vec = x_vec + (phi / rho) * w_vec
    w_vec = vec - (theta / rho) * w_vec
    return (x_vec, w_vec, phibar, rhobar)


def on_device(blocks, block_rows, block_cols, block_valid, rhs):
    mats = blocks[0, 0]
    me = lax.axis_index("core")
    swap = [(0, 1), (1, 0)]
    count = 2 * HALF
    tile, rows_tile = array(count, W), array(PAD, W)
    copied, wide = array(CBL, count, W), array(CBL, count + PAD, W)
    halved = jax.ShapeDtypeStruct(mats.shape, BF16)

    def exchange(x, axis):
        return lax.all_to_all(x, axis, 0, 0, tiled=True)

    def other_core(x):
        return lax.ppermute(x, "core", swap)

    def in_order(mine, other):
        return jnp.concatenate([jnp.where(me == 0, mine, other), jnp.where(me == 0, other, mine)])

    def scratch(sources, targets):
        return (pltpu.VMEM((sources, HALF, 2 * W), BF16), pltpu.VMEM((targets + 1, HALF, W), F32))

    pieces = rhs[0, 0].reshape(2, HALF, W)
    mine = jnp.where(me == 0, pieces[0], pieces[1])
    rest = jnp.where(me == 0, pieces[1], pieces[0])
    own_slots = jnp.stack([block_rows[0, 0], block_cols[0, 0], block_valid[0, 0]])
    listed = jnp.pad(own_slots.astype(F32), ((0, PAD - 3), (0, W - SLOTS)))
    got = other_core(jnp.concatenate([rest, listed]))
    slots = (own_slots, got[HALF : HALF + 3, :SLOTS].astype(jnp.int32))
    piece = in_order(mine, got[:HALF])
    other_mats, _ = lax.optimization_barrier((mats, got))
    other_mats = other_core(other_mats)
    specs = [SMEM] * 2 + [VMEM] * 5

    def first_backward():
        full = lax.all_gather(piece, "z")
        outs = (wide,) + (halved,) * 8
        held = (pltpu.VMEM((2, SLOTS, W, W), F32), pltpu.SemaphoreType.DMA((2 * SLOTS // GROUP,)))
        in_specs = [SMEM] * 2 + [ANY] * 2 + [VMEM]
        apply = call(first_backward_kernel, "apply_first", in_specs, outs, held + scratch(RBL, 2 * CBL))
        part, hi0, lo0, hi_t0, lo_t0, hi1, lo1, hi_t1, lo_t1 = apply(*slots, mats, other_mats, full)
        return exchange(part, "row"), full, (hi0, lo0, hi1, lo1), (hi_t0, lo_t0, hi_t1, lo_t1)

    def backward(fresh):
        full = lax.all_gather(fresh, "z")
        apply = call(backward_kernel, "apply_transposed", specs, (wide, tile, tile), scratch(RBL, 2 * CBL))
        part, alpha, factor = apply(*slots, *plain, full)
        return exchange(part, "row"), full, alpha, factor

    def forward(copies, full, first, second):
        vec = exchange(copies, "row")
        apply = call(
            forward_kernel, "apply_plain", specs + [VMEM] * 3, (copied, rows_tile), scratch(2 * CBL, RBL)
        )
        part, norms = apply(*slots, *turned, vec, full, first, second)
        return exchange(part, "z"), norms

    def everywhere(row):
        copies = jnp.broadcast_to(row[None], (ROWS * NZ, 1, W))
        return jnp.sum(exchange(copies, ("row", "z")), axis=0)

    got, full, plain, turned = first_backward()
    outs = (copied, tile, tile, tile)
    copies, v_old, beta, second = call(first_cols_kernel, "first_cols", [VMEM], outs)(got)
    u_old, first = piece, jnp.ones((count, W), F32)
    state = None
    for step_index in range(ITERS):
        got, norms = forward(copies, full, first, second)
        fresh = call(rows_kernel, "rows", [VMEM] * 5, array(count + PAD, W))(got, u_old, first, second, norms)
        got, full, alpha, first = backward(fresh)
        u_old = fresh
        if step_index == ITERS - 1:
            last = everywhere(call(squares_kernel, "squares", [VMEM], array(1, W))(fresh))
            alpha, last_beta = call(last_kernel, "last", [VMEM], (tile, tile))(last)
        v_now = v_old / alpha
        if state is None:
            state = (jnp.zeros_like(v_now), v_now, beta, alpha)
        else:
            state = advance(state, v_now, alpha, beta)
        copies, v_old, beta, second = call(cols_kernel, "cols", [VMEM] * 3, outs)(got, v_old, alpha)
    squares = jnp.sum(v_old * v_old, axis=1)
    squares = squares[:HALF] + squares[HALF:]
    total = everywhere(jnp.pad(squares, (0, W - HALF))[None])
    alpha = call(total_kernel, "total", [VMEM], tile)(total)
    x_vec = advance(state, v_old / alpha, alpha, last_beta)[0]
    return in_order(x_vec[:HALF], other_core(x_vec[HALF:]))[None, None]


def solution(mesh):
    grid = Mesh(mesh.devices.reshape(16, NZ, 2), ("row", "z", "core"))
    col = ("z", "core")
    placed = (
        P("row", col, None, None, None),
        P("row", col, None),
        P("row", col, None),
        P("row", col, None),
        P("row", col, None, None),
    )
    return jax.shard_map(
        on_device,
        mesh=grid,
        in_specs=placed,
        out_specs=P("row", col, None, None),
        check_vma=False,
    )
```

```python
import jax
import jax.numpy as jnp
from jax import lax
from jax.experimental import pallas as pl
from jax.experimental.pallas import tpu as pltpu
from jax.sharding import Mesh, PartitionSpec as P

W = 128
SLOTS = 64
GROUP = 16
HALF = 32
RBL = 32
CBL = 16
NZ = 16
ROWS = 16
ITERS = 2
PAD = 8
eps = 1e-06
SCALE = 0.25
TINY = 2.0**-64
LARGE = 1e37

F32 = jnp.float32
BF16 = jnp.bfloat16

SMEM = pl.BlockSpec(memory_space=pltpu.SMEM)
VMEM = pl.BlockSpec(memory_space=pltpu.VMEM)
HBM = pl.BlockSpec(memory_space=pltpu.HBM)
PARAMS = pltpu.CompilerParams(vmem_limit_bytes=16 << 20)


def root(total):
    return jnp.sqrt(total + eps)


def halves(x):
    hi = x.astype(BF16)
    return hi, (x - hi.astype(F32)).astype(BF16)


def diagonal(count):
    shape = (count, W)
    return lax.broadcasted_iota(jnp.int32, shape, 0) == lax.broadcasted_iota(jnp.int32, shape, 1)


def to_row(col):
    return jnp.sum(jnp.where(diagonal(col.shape[0]), col, 0.0), axis=0, keepdims=True)


def to_col(row, count):
    return jnp.sum(jnp.where(diagonal(count), row, 0.0), axis=1, keepdims=True)


def spread(col):
    return jnp.broadcast_to(col, (col.shape[0], W))


def per_vector(squares):
    total = jnp.sum(squares, axis=1, keepdims=True)
    total = total[:HALF] + total[HALF:]
    return jnp.concatenate([total, total], axis=0)


def norm_rows(squares):
    return jnp.broadcast_to(to_row(per_vector(squares)), (PAD, W))


def add_product(slots, s, side, high, low, parts, acc, source, target, unused):
    both = jnp.concatenate([high, low], axis=1)
    prod = jnp.dot(parts[source(side, slots, s)], both, preferred_element_type=F32)
    prod = prod[:HALF, :W] + (prod[HALF:, :W] + prod[:HALF, W:])
    acc[jnp.where(slots[2, s] > 0, target(side, slots, s), unused)] += prod


def products(sides, parts, acc, source, target, unused):
    acc[...] = jnp.zeros_like(acc)
    for side, (slots, hi, lo) in enumerate(sides):
        for s in range(SLOTS):
            add_product(slots, s, side, hi[s], lo[s], parts, acc, source, target, unused)


def by_row(side, slots, s):
    return slots[0, s]


def by_col(side, slots, s):
    return slots[1, s] + side * CBL


def store_tiles(parts, first, second, x):
    hi, lo = halves(x * SCALE)
    parts[first] = jnp.concatenate([hi[:HALF], lo[:HALF]], axis=0)
    parts[second] = jnp.concatenate([hi[HALF:], lo[HALF:]], axis=0)


def emit_cols(out, acc, squares):
    norms = norm_rows(squares)
    for c in range(CBL):
        out[c, :HALF] = acc[c]
        out[c, HALF : 2 * HALF] = acc[CBL + c]
        out[c, 2 * HALF :] = norms


def first_backward_kernel(slots0, slots1, mats0, mats1, vec, out, *rest):
    kept, (blocks, arrived, parts, acc) = rest[:8], rest[8:]
    copies = []
    for index in range(SLOTS // GROUP):
        some = pl.ds(index * GROUP, GROUP)
        copies.append(pltpu.make_async_copy(mats0.at[some], blocks.at[some], arrived.at[index]))
        copies[index].start()
    squares = jnp.zeros((2 * HALF, W), F32)
    for z in range(NZ):
        x = vec[z]
        squares += x * x
        store_tiles(parts, 2 * z, 2 * z + 1, x)
    acc[...] = jnp.zeros_like(acc)
    for side, slots, mats in ((1, slots1, mats1), (0, slots0, blocks)):
        hi, lo, hi_t, lo_t = kept[4 * side : 4 * side + 4]
        for s in range(SLOTS):
            if side == 0 and s % GROUP == 0:
                copies[s // GROUP].wait()
            block = mats[s]
            high, low = halves(block)
            hi[s], lo[s] = high, low
            hi_t[s], lo_t[s] = halves(block.T)
            add_product(slots, s, side, high, low, parts, acc, by_row, by_col, 2 * CBL)
    emit_cols(out, acc, squares)


def backward_kernel(slots0, slots1, hi0, lo0, hi1, lo1, vec, out, scale, factor, parts, acc):
    count = 2 * HALF
    total = jnp.zeros((PAD, W), F32)
    for z in range(NZ):
        total += vec[z, count:]
    alpha = root(to_col(total[:1], count))
    scale[...] = spread(alpha)
    inverse = spread(1.0 / (SCALE * alpha))
    factor[...] = inverse
    squares = jnp.zeros((count, W), F32)
    for z in range(NZ):
        x = vec[z, :count] * inverse
        squares += x * x
        store_tiles(parts, 2 * z, 2 * z + 1, x)
    sides = ((slots0, hi0, lo0), (slots1, hi1, lo1))
    products(sides, parts, acc, by_row, by_col, 2 * CBL)
    emit_cols(out, acc, squares)


def forward_kernel(slots0, slots1, hi0, lo0, hi1, lo1, vec, old, first, second, out, norms, parts, acc):
    count = 2 * HALF
    squares = jnp.zeros((count, W), F32)
    for c in range(CBL):
        x = vec[c]
        squares += x * x
        store_tiles(parts, c, CBL + c, x)
    sides = ((slots0, hi0, lo0), (slots1, hi1, lo1))
    products(sides, parts, acc, by_col, by_row, RBL)
    norms[...] = norm_rows(squares)
    weight = SCALE * spread(per_vector(squares))
    for z in range(NZ):
        less = weight * ((old[z, :count] * first[...]) * second[...])
        out[z, :HALF] = acc[2 * z] - less[:HALF]
        out[z, HALF:] = acc[2 * z + 1] - less[HALF:]


def summed(got):
    total = got[0]
    for index in range(1, got.shape[0]):
        total += got[index]
    return total


def first_cols_kernel(got, copies, fresh, scale, inverse):
    count = fresh.shape[0]
    total = summed(got)
    beta = root(to_col(total[count : count + 1], count))
    vec = total[:count] / (SCALE * beta)
    fresh[...] = vec
    copies[...] = jnp.broadcast_to(vec[None], copies.shape)
    scale[...] = spread(beta)
    inverse[...] = spread(1.0 / beta)


def cols_kernel(got, old, alpha, copies, fresh, scale, inverse):
    count = fresh.shape[0]
    total = summed(got)
    beta = root(to_col(total[count : count + 1], count))
    vec = total[:count] / (SCALE * beta) - beta * (old[...] / alpha[...])
    fresh[...] = vec
    copies[...] = jnp.broadcast_to(vec[None], copies.shape)
    scale[...] = spread(beta)
    inverse[...] = spread(1.0 / beta)


def rows_kernel(got, old, first, second, norms, fresh):
    count = first.shape[0]
    fresh[:count] = summed(got) - (SCALE * eps) * ((old[:count] * first[...]) * second[...])
    fresh[count:] = norms[...]


def lanes(start):
    shape = (2 * HALF, W)
    vector = lax.rem(lax.broadcasted_iota(jnp.int32, shape, 0), HALF)
    return lax.broadcasted_iota(jnp.int32, shape, 1) == vector + start


def row_at(squares, start):
    return jnp.sum(jnp.where(lanes(start), jnp.sum(squares, axis=1, keepdims=True), 0.0), axis=0, keepdims=True)


def col_at(row, start):
    return jnp.sum(jnp.where(lanes(start), row, 0.0), axis=1, keepdims=True)


def squares_kernel(piece, out):
    count = 2 * HALF
    vec = piece[:count]
    small = vec * TINY
    norms = col_at(piece[count : count + 1], 0) * (0.5 / ROWS)
    norms = jnp.sum(jnp.where(lanes(2 * HALF), norms, 0.0), axis=0, keepdims=True)
    out[...] = row_at(vec * vec, 0) + row_at(small * small, HALF) + norms


def last_kernel(got, scale_alpha, scale_beta):
    total = got[...]
    alpha = root(col_at(total, 2 * HALF))
    plain, small = col_at(total, 0), col_at(total, HALF)
    norm = jnp.where(plain < LARGE, jnp.sqrt(plain), jnp.sqrt(small) / TINY)
    norm = norm / (SCALE * alpha)
    scale_alpha[...] = spread(alpha)
    scale_beta[...] = spread(root(norm * norm))


def total_kernel(got, scale):
    scale[...] = spread(root(col_at(got[...], 0)))


def call(kernel, name, specs, outs, scratch=()):
    return pl.pallas_call(
        kernel,
        out_shape=outs,
        in_specs=specs,
        out_specs=jax.tree.map(lambda _: VMEM, outs),
        scratch_shapes=scratch,
        compiler_params=PARAMS,
        name=name,
    )


def array(*shape):
    return jax.ShapeDtypeStruct(shape, F32)


def advance(state, vec, alpha, beta):
    x_vec, w_vec, phibar, rhobar = state
    rho = jnp.sqrt(rhobar * rhobar + beta * beta)
    cosine = rhobar / rho
    sine = beta / rho
    theta = sine * alpha
    rhobar = -cosine * alpha
    phi = cosine * phibar
    phibar = sine * phibar
    x_vec = x_vec + (phi / rho) * w_vec
    w_vec = vec - (theta / rho) * w_vec
    return (x_vec, w_vec, phibar, rhobar)


def on_device(blocks, block_rows, block_cols, block_valid, rhs):
    mats = blocks[0, 0]
    me = lax.axis_index("core")
    swap = [(0, 1), (1, 0)]
    count = 2 * HALF
    tile, rows_tile = array(count, W), array(PAD, W)
    copied, wide = array(CBL, count, W), array(CBL, count + PAD, W)
    halved = jax.ShapeDtypeStruct(mats.shape, BF16)

    def exchange(x, axis):
        return lax.all_to_all(x, axis, 0, 0, tiled=True)

    def other_core(x):
        return lax.ppermute(x, "core", swap)

    def in_order(mine, other):
        return jnp.concatenate([jnp.where(me == 0, mine, other), jnp.where(me == 0, other, mine)])

    def scratch(sources, targets):
        return (pltpu.VMEM((sources, 2 * HALF, W), BF16), pltpu.VMEM((targets + 1, HALF, W), F32))

    pieces = rhs[0, 0].reshape(2, HALF, W)
    mine = jnp.where(me == 0, pieces[0], pieces[1])
    rest = jnp.where(me == 0, pieces[1], pieces[0])
    own_slots = jnp.stack([block_rows[0, 0], block_cols[0, 0], block_valid[0, 0]])
    listed = jnp.pad(own_slots.astype(F32), ((0, PAD - 3), (0, W - SLOTS)))
    got = other_core(jnp.concatenate([rest, listed]))
    slots = (own_slots, got[HALF : HALF + 3, :SLOTS].astype(jnp.int32))
    piece = in_order(mine, got[:HALF])
    other_mats, _ = lax.optimization_barrier((mats, got))
    other_mats = other_core(other_mats)
    specs = [SMEM] * 2 + [VMEM] * 5

    def first_backward():
        full = lax.all_gather(piece, "z")
        outs = (wide,) + (halved,) * 8
        held = (pltpu.VMEM((SLOTS, W, W), F32), pltpu.SemaphoreType.DMA((SLOTS // GROUP,)))
        in_specs = [SMEM] * 2 + [HBM] + [VMEM] * 2
        apply = call(first_backward_kernel, "apply_first", in_specs, outs, held + scratch(RBL, 2 * CBL))
        part, hi0, lo0, hi_t0, lo_t0, hi1, lo1, hi_t1, lo_t1 = apply(*slots, mats, other_mats, full)
        return exchange(part, "row"), full, (hi0, lo0, hi1, lo1), (hi_t0, lo_t0, hi_t1, lo_t1)

    def backward(fresh):
        full = lax.all_gather(fresh, "z")
        apply = call(backward_kernel, "apply_transposed", specs, (wide, tile, tile), scratch(RBL, 2 * CBL))
        part, alpha, factor = apply(*slots, *plain, full)
        return exchange(part, "row"), full, alpha, factor

    def forward(copies, full, first, second):
        vec = exchange(copies, "row")
        apply = call(
            forward_kernel, "apply_plain", specs + [VMEM] * 3, (copied, rows_tile), scratch(2 * CBL, RBL)
        )
        part, norms = apply(*slots, *turned, vec, full, first, second)
        return exchange(part, "z"), norms

    def everywhere(row):
        copies = jnp.broadcast_to(row[None], (ROWS * NZ, 1, W))
        return jnp.sum(exchange(copies, ("row", "z")), axis=0)

    got, full, plain, turned = first_backward()
    outs = (copied, tile, tile, tile)
    copies, v_old, beta, second = call(first_cols_kernel, "first_cols", [VMEM], outs)(got)
    u_old, first = piece, jnp.ones((count, W), F32)
    state = None
    for step_index in range(ITERS):
        got, norms = forward(copies, full, first, second)
        fresh = call(rows_kernel, "rows", [VMEM] * 5, array(count + PAD, W))(got, u_old, first, second, norms)
        got, full, alpha, first = backward(fresh)
        u_old = fresh
        if step_index == ITERS - 1:
            last = everywhere(call(squares_kernel, "squares", [VMEM], array(1, W))(fresh))
            alpha, last_beta = call(last_kernel, "last", [VMEM], (tile, tile))(last)
        v_now = v_old / alpha
        if state is None:
            state = (jnp.zeros_like(v_now), v_now, beta, alpha)
        else:
            state = advance(state, v_now, alpha, beta)
        copies, v_old, beta, second = call(cols_kernel, "cols", [VMEM] * 3, outs)(got, v_old, alpha)
    squares = jnp.sum(v_old * v_old, axis=1)
    squares = squares[:HALF] + squares[HALF:]
    total = everywhere(jnp.pad(squares, (0, W - HALF))[None])
    alpha = call(total_kernel, "total", [VMEM], tile)(total)
    x_vec = advance(state, v_old / alpha, alpha, last_beta)[0]
    return in_order(x_vec[:HALF], other_core(x_vec[HALF:]))[None, None]


def solution(mesh):
    grid = Mesh(mesh.devices.reshape(16, NZ, 2), ("row", "z", "core"))
    col = ("z", "core")
    placed = (
        P("row", col, None, None, None),
        P("row", col, None),
        P("row", col, None),
        P("row", col, None),
        P("row", col, None, None),
    )
    return jax.shard_map(
        on_device,
        mesh=grid,
        in_specs=placed,
        out_specs=P("row", col, None, None),
        check_vma=False,
    )
```

```python
import jax
import jax.numpy as jnp
from jax import lax
from jax.experimental import pallas as pl
from jax.experimental.pallas import tpu as pltpu
from jax.sharding import Mesh, PartitionSpec as P

W = 128
SLOTS = 64
HALF = 32
RBL = 32
CBL = 16
NZ = 16
ROWS = 16
ITERS = 2
PAD = 8
eps = 1e-06
SCALE = 0.25
TINY = 2.0**-64
LARGE = 1e37

F32 = jnp.float32
BF16 = jnp.bfloat16

SMEM = pl.BlockSpec(memory_space=pltpu.SMEM)
VMEM = pl.BlockSpec(memory_space=pltpu.VMEM)
PARAMS = pltpu.CompilerParams(vmem_limit_bytes=16 << 20)


def root(total):
    return jnp.sqrt(total + eps)


def halves(x):
    hi = x.astype(BF16)
    return hi, (x - hi.astype(F32)).astype(BF16)


def diagonal(count):
    shape = (count, W)
    return lax.broadcasted_iota(jnp.int32, shape, 0) == lax.broadcasted_iota(jnp.int32, shape, 1)


def to_row(col):
    return jnp.sum(jnp.where(diagonal(col.shape[0]), col, 0.0), axis=0, keepdims=True)


def to_col(row, count):
    return jnp.sum(jnp.where(diagonal(count), row, 0.0), axis=1, keepdims=True)


def spread(col):
    return jnp.broadcast_to(col, (col.shape[0], W))


def per_vector(squares):
    total = jnp.sum(squares, axis=1, keepdims=True)
    total = total[:HALF] + total[HALF:]
    return jnp.concatenate([total, total], axis=0)


def norm_rows(squares):
    return jnp.broadcast_to(to_row(per_vector(squares)), (PAD, W))


def add_product(slots, s, side, high, low, parts, acc, source, target, unused):
    both = jnp.concatenate([high, low], axis=1)
    prod = jnp.dot(parts[source(side, slots, s)], both, preferred_element_type=F32)
    prod = prod[:HALF, :W] + (prod[HALF:, :W] + prod[:HALF, W:])
    acc[jnp.where(slots[2, s] > 0, target(side, slots, s), unused)] += prod


def products(sides, parts, acc, source, target, unused):
    acc[...] = jnp.zeros_like(acc)
    for side, (slots, hi, lo) in enumerate(sides):
        for s in range(SLOTS):
            add_product(slots, s, side, hi[s], lo[s], parts, acc, source, target, unused)


def by_row(side, slots, s):
    return slots[0, s]


def by_col(side, slots, s):
    return slots[1, s] + side * CBL


def store_tiles(parts, first, second, x):
    hi, lo = halves(x * SCALE)
    parts[first] = jnp.concatenate([hi[:HALF], lo[:HALF]], axis=0)
    parts[second] = jnp.concatenate([hi[HALF:], lo[HALF:]], axis=0)


def emit_cols(out, acc, squares):
    norms = norm_rows(squares)
    for c in range(CBL):
        out[c, :HALF] = acc[c]
        out[c, HALF : 2 * HALF] = acc[CBL + c]
        out[c, 2 * HALF :] = norms


def first_products(slots, mats, kept, parts, acc):
    hi, lo, hi_t, lo_t = kept
    acc[...] = jnp.zeros_like(acc)
    for s in range(SLOTS):
        block = mats[s]
        high, low = halves(block)
        hi[s], lo[s] = high, low
        hi_t[s], lo_t[s] = halves(block.T)
        add_product(slots, s, 0, high, low, parts, acc, by_row, by_col, CBL)


def first_other_kernel(slots, mats, vec, hi, lo, hi_t, lo_t, parts, part, norms, acc):
    squares = jnp.zeros((2 * HALF, W), F32)
    for z in range(NZ):
        x = vec[z]
        squares += x * x
        store_tiles(parts, 2 * z, 2 * z + 1, x)
    norms[...] = norm_rows(squares)
    first_products(slots, mats, (hi, lo, hi_t, lo_t), parts, acc)
    part[...] = acc[:CBL]


def first_own_kernel(slots, mats, parts, part, norms, hi, lo, hi_t, lo_t, out, acc):
    first_products(slots, mats, (hi, lo, hi_t, lo_t), parts, acc)
    for c in range(CBL):
        out[c, :HALF] = acc[c]
        out[c, HALF : 2 * HALF] = part[c]
        out[c, 2 * HALF :] = norms[...]


def backward_kernel(slots0, slots1, hi0, lo0, hi1, lo1, vec, out, scale, factor, parts, acc):
    count = 2 * HALF
    total = jnp.zeros((PAD, W), F32)
    for z in range(NZ):
        total += vec[z, count:]
    alpha = root(to_col(total[:1], count))
    scale[...] = spread(alpha)
    inverse = spread(1.0 / (SCALE * alpha))
    factor[...] = inverse
    squares = jnp.zeros((count, W), F32)
    for z in range(NZ):
        x = vec[z, :count] * inverse
        squares += x * x
        store_tiles(parts, 2 * z, 2 * z + 1, x)
    sides = ((slots0, hi0, lo0), (slots1, hi1, lo1))
    products(sides, parts, acc, by_row, by_col, 2 * CBL)
    emit_cols(out, acc, squares)


def forward_kernel(slots0, slots1, hi0, lo0, hi1, lo1, vec, old, first, second, out, norms, parts, acc):
    count = 2 * HALF
    squares = jnp.zeros((count, W), F32)
    for c in range(CBL):
        x = vec[c]
        squares += x * x
        store_tiles(parts, c, CBL + c, x)
    sides = ((slots0, hi0, lo0), (slots1, hi1, lo1))
    products(sides, parts, acc, by_col, by_row, RBL)
    norms[...] = norm_rows(squares)
    weight = SCALE * spread(per_vector(squares))
    for z in range(NZ):
        less = weight * ((old[z, :count] * first[...]) * second[...])
        out[z, :HALF] = acc[2 * z] - less[:HALF]
        out[z, HALF:] = acc[2 * z + 1] - less[HALF:]


def summed(got):
    total = got[0]
    for index in range(1, got.shape[0]):
        total += got[index]
    return total


def first_cols_kernel(got, copies, fresh, scale, inverse):
    count = fresh.shape[0]
    total = summed(got)
    beta = root(to_col(total[count : count + 1], count))
    vec = total[:count] / (SCALE * beta)
    fresh[...] = vec
    copies[...] = jnp.broadcast_to(vec[None], copies.shape)
    scale[...] = spread(beta)
    inverse[...] = spread(1.0 / beta)


def cols_kernel(got, old, alpha, copies, fresh, scale, inverse):
    count = fresh.shape[0]
    total = summed(got)
    beta = root(to_col(total[count : count + 1], count))
    vec = total[:count] / (SCALE * beta) - beta * (old[...] / alpha[...])
    fresh[...] = vec
    copies[...] = jnp.broadcast_to(vec[None], copies.shape)
    scale[...] = spread(beta)
    inverse[...] = spread(1.0 / beta)


def rows_kernel(got, old, first, second, norms, fresh):
    count = first.shape[0]
    fresh[:count] = summed(got) - (SCALE * eps) * ((old[:count] * first[...]) * second[...])
    fresh[count:] = norms[...]


def lanes(start):
    shape = (2 * HALF, W)
    vector = lax.rem(lax.broadcasted_iota(jnp.int32, shape, 0), HALF)
    return lax.broadcasted_iota(jnp.int32, shape, 1) == vector + start


def row_at(squares, start):
    return jnp.sum(jnp.where(lanes(start), jnp.sum(squares, axis=1, keepdims=True), 0.0), axis=0, keepdims=True)


def col_at(row, start):
    return jnp.sum(jnp.where(lanes(start), row, 0.0), axis=1, keepdims=True)


def squares_kernel(piece, out):
    count = 2 * HALF
    vec = piece[:count]
    small = vec * TINY
    norms = col_at(piece[count : count + 1], 0) * (0.5 / ROWS)
    norms = jnp.sum(jnp.where(lanes(2 * HALF), norms, 0.0), axis=0, keepdims=True)
    out[...] = row_at(vec * vec, 0) + row_at(small * small, HALF) + norms


def last_kernel(got, scale_alpha, scale_beta):
    total = got[...]
    alpha = root(col_at(total, 2 * HALF))
    plain, small = col_at(total, 0), col_at(total, HALF)
    norm = jnp.where(plain < LARGE, jnp.sqrt(plain), jnp.sqrt(small) / TINY)
    norm = norm / (SCALE * alpha)
    scale_alpha[...] = spread(alpha)
    scale_beta[...] = spread(root(norm * norm))


def total_kernel(got, scale):
    scale[...] = spread(root(col_at(got[...], 0)))


def call(kernel, name, specs, outs, scratch=(), cost=None):
    return pl.pallas_call(
        kernel,
        out_shape=outs,
        in_specs=specs,
        out_specs=jax.tree.map(lambda _: VMEM, outs),
        scratch_shapes=scratch,
        compiler_params=PARAMS,
        cost_estimate=cost,
        name=name,
    )


def array(*shape):
    return jax.ShapeDtypeStruct(shape, F32)


def advance(state, vec, alpha, beta):
    x_vec, w_vec, phibar, rhobar = state
    rho = jnp.sqrt(rhobar * rhobar + beta * beta)
    cosine = rhobar / rho
    sine = beta / rho
    theta = sine * alpha
    rhobar = -cosine * alpha
    phi = cosine * phibar
    phibar = sine * phibar
    x_vec = x_vec + (phi / rho) * w_vec
    w_vec = vec - (theta / rho) * w_vec
    return (x_vec, w_vec, phibar, rhobar)


def on_device(blocks, block_rows, block_cols, block_valid, rhs):
    mats = blocks[0, 0]
    me = lax.axis_index("core")
    swap = [(0, 1), (1, 0)]
    count = 2 * HALF
    tile, rows_tile = array(count, W), array(PAD, W)
    copied, wide = array(CBL, count, W), array(CBL, count + PAD, W)
    halved = jax.ShapeDtypeStruct(mats.shape, BF16)

    def exchange(x, axis):
        return lax.all_to_all(x, axis, 0, 0, tiled=True)

    def other_core(x):
        return lax.ppermute(x, "core", swap)

    def in_order(mine, other):
        return jnp.concatenate([jnp.where(me == 0, mine, other), jnp.where(me == 0, other, mine)])

    def scratch(sources, targets):
        return (pltpu.VMEM((sources, 2 * HALF, W), BF16), pltpu.VMEM((targets + 1, HALF, W), F32))

    pieces = rhs[0, 0].reshape(2, HALF, W)
    mine = jnp.where(me == 0, pieces[0], pieces[1])
    rest = jnp.where(me == 0, pieces[1], pieces[0])
    own_slots = jnp.stack([block_rows[0, 0], block_cols[0, 0], block_valid[0, 0]])
    listed = jnp.pad(own_slots.astype(F32), ((0, PAD - 3), (0, W - SLOTS)))
    got = other_core(jnp.concatenate([rest, listed]))
    slots = (own_slots, got[HALF : HALF + 3, :SLOTS].astype(jnp.int32))
    piece = in_order(mine, got[:HALF])
    other_mats, _ = lax.optimization_barrier((mats, got))
    other_mats = other_core(other_mats)
    specs = [SMEM] * 2 + [VMEM] * 5

    def first_backward():
        full = lax.all_gather(piece, "z")
        parts = jax.ShapeDtypeStruct((RBL, 2 * HALF, W), BF16)
        acc = (pltpu.VMEM((CBL + 1, HALF, W), F32),)
        outs = (halved,) * 4 + (parts, array(CBL, HALF, W), rows_tile)
        cost = pl.CostEstimate(flops=SLOTS * 2**22, bytes_accessed=SLOTS * 3 * 2**16, transcendentals=0)
        apply = call(first_other_kernel, "apply_first_other", [SMEM] + [VMEM] * 2, outs, acc, cost)
        *kept1, parts, part, norms = apply(slots[1], other_mats, full)
        outs = (halved,) * 4 + (wide,)
        apply = call(first_own_kernel, "apply_first_own", [SMEM] + [VMEM] * 4, outs, acc, cost)
        *kept0, out = apply(slots[0], mats, parts, part, norms)
        return exchange(out, "row"), full, (*kept0[:2], *kept1[:2]), (*kept0[2:], *kept1[2:])

    def backward(fresh):
        full = lax.all_gather(fresh, "z")
        apply = call(backward_kernel, "apply_transposed", specs, (wide, tile, tile), scratch(RBL, 2 * CBL))
        part, alpha, factor = apply(*slots, *plain, full)
        return exchange(part, "row"), full, alpha, factor

    def forward(copies, full, first, second):
        vec = exchange(copies, "row")
        apply = call(
            forward_kernel, "apply_plain", specs + [VMEM] * 3, (copied, rows_tile), scratch(2 * CBL, RBL)
        )
        part, norms = apply(*slots, *turned, vec, full, first, second)
        return exchange(part, "z"), norms

    def everywhere(row):
        copies = jnp.broadcast_to(row[None], (ROWS * NZ, 1, W))
        return jnp.sum(exchange(copies, ("row", "z")), axis=0)

    got, full, plain, turned = first_backward()
    outs = (copied, tile, tile, tile)
    copies, v_old, beta, second = call(first_cols_kernel, "first_cols", [VMEM], outs)(got)
    u_old, first = piece, jnp.ones((count, W), F32)
    state = None
    for step_index in range(ITERS):
        got, norms = forward(copies, full, first, second)
        fresh = call(rows_kernel, "rows", [VMEM] * 5, array(count + PAD, W))(got, u_old, first, second, norms)
        got, full, alpha, first = backward(fresh)
        u_old = fresh
        if step_index == ITERS - 1:
            last = everywhere(call(squares_kernel, "squares", [VMEM], array(1, W))(fresh))
            alpha, last_beta = call(last_kernel, "last", [VMEM], (tile, tile))(last)
        v_now = v_old / alpha
        if state is None:
            state = (jnp.zeros_like(v_now), v_now, beta, alpha)
        else:
            state = advance(state, v_now, alpha, beta)
        copies, v_old, beta, second = call(cols_kernel, "cols", [VMEM] * 3, outs)(got, v_old, alpha)
    squares = jnp.sum(v_old * v_old, axis=1)
    squares = squares[:HALF] + squares[HALF:]
    total = everywhere(jnp.pad(squares, (0, W - HALF))[None])
    alpha = call(total_kernel, "total", [VMEM], tile)(total)
    x_vec = advance(state, v_old / alpha, alpha, last_beta)[0]
    return in_order(x_vec[:HALF], other_core(x_vec[HALF:]))[None, None]


def solution(mesh):
    grid = Mesh(mesh.devices.reshape(16, NZ, 2), ("row", "z", "core"))
    col = ("z", "core")
    placed = (
        P("row", col, None, None, None),
        P("row", col, None),
        P("row", col, None),
        P("row", col, None),
        P("row", col, None, None),
    )
    return jax.shard_map(
        on_device,
        mesh=grid,
        in_specs=placed,
        out_specs=P("row", col, None, None),
        check_vma=False,
    )
```

```python
import jax
import jax.numpy as jnp
from jax import lax
from jax.experimental import pallas as pl
from jax.experimental.pallas import tpu as pltpu
from jax.sharding import Mesh, PartitionSpec as P

W = 128
SLOTS = 64
HALF = 32
RBL = 32
CBL = 16
NZ = 16
ROWS = 16
ITERS = 2
PAD = 8
eps = 1e-06
SCALE = 0.25
TINY = 2.0**-64
LARGE = 1e37

F32 = jnp.float32
BF16 = jnp.bfloat16

SMEM = pl.BlockSpec(memory_space=pltpu.SMEM)
VMEM = pl.BlockSpec(memory_space=pltpu.VMEM)
PARAMS = pltpu.CompilerParams(vmem_limit_bytes=16 << 20)


def root(total):
    return jnp.sqrt(total + eps)


def halves(x):
    hi = x.astype(BF16)
    return hi, (x - hi.astype(F32)).astype(BF16)


def diagonal(count):
    shape = (count, W)
    return lax.broadcasted_iota(jnp.int32, shape, 0) == lax.broadcasted_iota(jnp.int32, shape, 1)


def to_row(col):
    return jnp.sum(jnp.where(diagonal(col.shape[0]), col, 0.0), axis=0, keepdims=True)


def to_col(row, count):
    return jnp.sum(jnp.where(diagonal(count), row, 0.0), axis=1, keepdims=True)


def spread(col):
    return jnp.broadcast_to(col, (col.shape[0], W))


def per_vector(squares):
    total = jnp.sum(squares, axis=1, keepdims=True)
    total = total[:HALF] + total[HALF:]
    return jnp.concatenate([total, total], axis=0)


def norm_rows(squares):
    return jnp.broadcast_to(to_row(per_vector(squares)), (PAD, W))


def add_product(slots, s, side, high, low, parts, acc, source, target, unused):
    both = jnp.concatenate([high, low], axis=1)
    prod = jnp.dot(parts[source(side, slots, s)], both, preferred_element_type=F32)
    prod = prod[:HALF, :W] + (prod[HALF:, :W] + prod[:HALF, W:])
    acc[jnp.where(slots[2, s] > 0, target(side, slots, s), unused)] += prod


def products(sides, parts, acc, source, target, unused):
    acc[...] = jnp.zeros_like(acc)
    for side, (slots, hi, lo) in enumerate(sides):
        for s in range(SLOTS):
            add_product(slots, s, side, hi[s], lo[s], parts, acc, source, target, unused)


def by_row(side, slots, s):
    return slots[0, s]


def by_col(side, slots, s):
    return slots[1, s] + side * CBL


def store_tiles(parts, first, second, x):
    hi, lo = halves(x * SCALE)
    parts[first] = jnp.concatenate([hi[:HALF], lo[:HALF]], axis=0)
    parts[second] = jnp.concatenate([hi[HALF:], lo[HALF:]], axis=0)


def emit_cols(out, acc, squares):
    norms = norm_rows(squares)
    for c in range(CBL):
        out[c, :HALF] = acc[c]
        out[c, HALF : 2 * HALF] = acc[CBL + c]
        out[c, 2 * HALF :] = norms


def first_products(slots, mats, kept, parts, acc):
    hi, lo, hi_t, lo_t = kept
    acc[...] = jnp.zeros_like(acc)
    for s in range(SLOTS):
        block = mats[s]
        high, low = halves(block)
        hi[s], lo[s] = high, low
        hi_t[s], lo_t[s] = halves(block.T)
        add_product(slots, s, 0, high, low, parts, acc, by_row, by_col, CBL)


def pack_kernel(core, data, rows, cols, valid, mine, slots, message):
    me = core[0]
    mine[...] = data[pl.ds(pl.multiple_of(me * HALF, HALF), HALF)]
    message[:HALF] = data[pl.ds(pl.multiple_of((1 - me) * HALF, HALF), HALF)]
    message[HALF:] = jnp.zeros((PAD, W), F32)
    for index, values in enumerate((rows, cols, valid)):
        slots[index : index + 1] = values[...]
        message[HALF + index : HALF + index + 1, :SLOTS] = values[...].astype(F32)


def first_other_kernel(slots, mats, vec, hi, lo, hi_t, lo_t, parts, part, norms, acc):
    squares = jnp.zeros((2 * HALF, W), F32)
    for z in range(NZ):
        x = vec[z]
        squares += x * x
        store_tiles(parts, 2 * z, 2 * z + 1, x)
    norms[...] = norm_rows(squares)
    first_products(slots, mats, (hi, lo, hi_t, lo_t), parts, acc)
    part[...] = acc[:CBL]


def first_own_kernel(slots, mats, parts, part, norms, hi, lo, hi_t, lo_t, out, acc):
    first_products(slots, mats, (hi, lo, hi_t, lo_t), parts, acc)
    for c in range(CBL):
        out[c, :HALF] = acc[c]
        out[c, HALF : 2 * HALF] = part[c]
        out[c, 2 * HALF :] = norms[...]


def backward_kernel(slots0, slots1, hi0, lo0, hi1, lo1, vec, out, scale, factor, parts, acc):
    count = 2 * HALF
    total = jnp.zeros((PAD, W), F32)
    for z in range(NZ):
        total += vec[z, count:]
    alpha = root(to_col(total[:1], count))
    scale[...] = spread(alpha)
    inverse = spread(1.0 / (SCALE * alpha))
    factor[...] = inverse
    squares = jnp.zeros((count, W), F32)
    for z in range(NZ):
        x = vec[z, :count] * inverse
        squares += x * x
        store_tiles(parts, 2 * z, 2 * z + 1, x)
    sides = ((slots0, hi0, lo0), (slots1, hi1, lo1))
    products(sides, parts, acc, by_row, by_col, 2 * CBL)
    emit_cols(out, acc, squares)


def forward_kernel(slots0, slots1, hi0, lo0, hi1, lo1, vec, old, first, second, out, norms, parts, acc):
    count = 2 * HALF
    squares = jnp.zeros((count, W), F32)
    for c in range(CBL):
        x = vec[c]
        squares += x * x
        store_tiles(parts, c, CBL + c, x)
    sides = ((slots0, hi0, lo0), (slots1, hi1, lo1))
    products(sides, parts, acc, by_col, by_row, RBL)
    norms[...] = norm_rows(squares)
    weight = SCALE * spread(per_vector(squares))
    for z in range(NZ):
        less = weight * ((old[z, :count] * first[...]) * second[...])
        out[z, :HALF] = acc[2 * z] - less[:HALF]
        out[z, HALF:] = acc[2 * z + 1] - less[HALF:]


def summed(got):
    total = got[0]
    for index in range(1, got.shape[0]):
        total += got[index]
    return total


def first_cols_kernel(got, copies, fresh, scale, inverse):
    count = fresh.shape[0]
    total = summed(got)
    beta = root(to_col(total[count : count + 1], count))
    vec = total[:count] / (SCALE * beta)
    fresh[...] = vec
    copies[...] = jnp.broadcast_to(vec[None], copies.shape)
    scale[...] = spread(beta)
    inverse[...] = spread(1.0 / beta)


def cols_kernel(got, old, alpha, copies, fresh, scale, inverse):
    count = fresh.shape[0]
    total = summed(got)
    beta = root(to_col(total[count : count + 1], count))
    vec = total[:count] / (SCALE * beta) - beta * (old[...] / alpha[...])
    fresh[...] = vec
    copies[...] = jnp.broadcast_to(vec[None], copies.shape)
    scale[...] = spread(beta)
    inverse[...] = spread(1.0 / beta)


def rows_kernel(got, old, first, second, norms, fresh):
    count = first.shape[0]
    fresh[:count] = summed(got) - (SCALE * eps) * ((old[:count] * first[...]) * second[...])
    fresh[count:] = norms[...]


def lanes(start):
    shape = (2 * HALF, W)
    vector = lax.rem(lax.broadcasted_iota(jnp.int32, shape, 0), HALF)
    return lax.broadcasted_iota(jnp.int32, shape, 1) == vector + start


def row_at(squares, start):
    return jnp.sum(jnp.where(lanes(start), jnp.sum(squares, axis=1, keepdims=True), 0.0), axis=0, keepdims=True)


def col_at(row, start):
    return jnp.sum(jnp.where(lanes(start), row, 0.0), axis=1, keepdims=True)


def squares_kernel(piece, out):
    count = 2 * HALF
    vec = piece[:count]
    small = vec * TINY
    norms = col_at(piece[count : count + 1], 0) * (0.5 / ROWS)
    norms = jnp.sum(jnp.where(lanes(2 * HALF), norms, 0.0), axis=0, keepdims=True)
    out[...] = row_at(vec * vec, 0) + row_at(small * small, HALF) + norms


def last_kernel(got, scale_alpha, scale_beta):
    total = got[...]
    alpha = root(col_at(total, 2 * HALF))
    plain, small = col_at(total, 0), col_at(total, HALF)
    norm = jnp.where(plain < LARGE, jnp.sqrt(plain), jnp.sqrt(small) / TINY)
    norm = norm / (SCALE * alpha)
    scale_alpha[...] = spread(alpha)
    scale_beta[...] = spread(root(norm * norm))


def total_kernel(got, scale):
    scale[...] = spread(root(col_at(got[...], 0)))


def call(kernel, name, specs, outs, scratch=(), cost=None):
    return pl.pallas_call(
        kernel,
        out_shape=outs,
        in_specs=specs,
        out_specs=jax.tree.map(lambda _: VMEM, outs),
        scratch_shapes=scratch,
        compiler_params=PARAMS,
        cost_estimate=cost,
        name=name,
    )


def array(*shape):
    return jax.ShapeDtypeStruct(shape, F32)


def advance(state, vec, alpha, beta):
    x_vec, w_vec, phibar, rhobar = state
    rho = jnp.sqrt(rhobar * rhobar + beta * beta)
    cosine = rhobar / rho
    sine = beta / rho
    theta = sine * alpha
    rhobar = -cosine * alpha
    phi = cosine * phibar
    phibar = sine * phibar
    x_vec = x_vec + (phi / rho) * w_vec
    w_vec = vec - (theta / rho) * w_vec
    return (x_vec, w_vec, phibar, rhobar)


def on_device(blocks, block_rows, block_cols, block_valid, rhs):
    mats = blocks[0, 0]
    me = lax.axis_index("core")
    swap = [(0, 1), (1, 0)]
    count = 2 * HALF
    tile, rows_tile = array(count, W), array(PAD, W)
    copied, wide = array(CBL, count, W), array(CBL, count + PAD, W)
    halved = jax.ShapeDtypeStruct(mats.shape, BF16)

    def exchange(x, axis):
        return lax.all_to_all(x, axis, 0, 0, tiled=True)

    def other_core(x):
        return lax.ppermute(x, "core", swap)

    def in_order(mine, other):
        return jnp.concatenate([jnp.where(me == 0, mine, other), jnp.where(me == 0, other, mine)])

    def scratch(sources, targets):
        return (pltpu.VMEM((sources, 2 * HALF, W), BF16), pltpu.VMEM((targets + 1, HALF, W), F32))

    outs = (array(HALF, W), jax.ShapeDtypeStruct((3, SLOTS), jnp.int32), array(HALF + PAD, W))
    lists = (block_rows[0], block_cols[0], block_valid[0])
    pack = call(pack_kernel, "pack", [SMEM] + [VMEM] * 4, outs)
    mine, own_slots, message = pack(me.astype(jnp.int32).reshape(1), rhs[0, 0], *lists)
    got = other_core(message)
    slots = (own_slots, got[HALF : HALF + 3, :SLOTS].astype(jnp.int32))
    piece = in_order(mine, got[:HALF])
    other_mats, _ = lax.optimization_barrier((mats, got))
    other_mats = other_core(other_mats)
    specs = [SMEM] * 2 + [VMEM] * 5

    def first_backward():
        full = lax.all_gather(piece, "z")
        parts = jax.ShapeDtypeStruct((RBL, 2 * HALF, W), BF16)
        acc = (pltpu.VMEM((CBL + 1, HALF, W), F32),)
        outs = (halved,) * 4 + (parts, array(CBL, HALF, W), rows_tile)
        cost = pl.CostEstimate(flops=SLOTS * 2**22, bytes_accessed=SLOTS * 3 * 2**16, transcendentals=0)
        apply = call(first_other_kernel, "apply_first_other", [SMEM] + [VMEM] * 2, outs, acc, cost)
        *kept1, parts, part, norms = apply(slots[1], other_mats, full)
        outs = (halved,) * 4 + (wide,)
        apply = call(first_own_kernel, "apply_first_own", [SMEM] + [VMEM] * 4, outs, acc, cost)
        *kept0, out = apply(slots[0], mats, parts, part, norms)
        return exchange(out, "row"), full, (*kept0[:2], *kept1[:2]), (*kept0[2:], *kept1[2:])

    def backward(fresh):
        full = lax.all_gather(fresh, "z")
        apply = call(backward_kernel, "apply_transposed", specs, (wide, tile, tile), scratch(RBL, 2 * CBL))
        part, alpha, factor = apply(*slots, *plain, full)
        return exchange(part, "row"), full, alpha, factor

    def forward(copies, full, first, second):
        vec = exchange(copies, "row")
        apply = call(
            forward_kernel, "apply_plain", specs + [VMEM] * 3, (copied, rows_tile), scratch(2 * CBL, RBL)
        )
        part, norms = apply(*slots, *turned, vec, full, first, second)
        return exchange(part, "z"), norms

    def everywhere(row):
        copies = jnp.broadcast_to(row[None], (ROWS * NZ, 1, W))
        return jnp.sum(exchange(copies, ("row", "z")), axis=0)

    got, full, plain, turned = first_backward()
    outs = (copied, tile, tile, tile)
    copies, v_old, beta, second = call(first_cols_kernel, "first_cols", [VMEM], outs)(got)
    u_old, first = piece, jnp.ones((count, W), F32)
    state = None
    for step_index in range(ITERS):
        got, norms = forward(copies, full, first, second)
        fresh = call(rows_kernel, "rows", [VMEM] * 5, array(count + PAD, W))(got, u_old, first, second, norms)
        got, full, alpha, first = backward(fresh)
        u_old = fresh
        if step_index == ITERS - 1:
            last = everywhere(call(squares_kernel, "squares", [VMEM], array(1, W))(fresh))
            alpha, last_beta = call(last_kernel, "last", [VMEM], (tile, tile))(last)
        v_now = v_old / alpha
        if state is None:
            state = (jnp.zeros_like(v_now), v_now, beta, alpha)
        else:
            state = advance(state, v_now, alpha, beta)
        copies, v_old, beta, second = call(cols_kernel, "cols", [VMEM] * 3, outs)(got, v_old, alpha)
    squares = jnp.sum(v_old * v_old, axis=1)
    squares = squares[:HALF] + squares[HALF:]
    total = everywhere(jnp.pad(squares, (0, W - HALF))[None])
    alpha = call(total_kernel, "total", [VMEM], tile)(total)
    x_vec = advance(state, v_old / alpha, alpha, last_beta)[0]
    return in_order(x_vec[:HALF], other_core(x_vec[HALF:]))[None, None]


def solution(mesh):
    grid = Mesh(mesh.devices.reshape(16, NZ, 2), ("row", "z", "core"))
    col = ("z", "core")
    placed = (
        P("row", col, None, None, None),
        P("row", col, None),
        P("row", col, None),
        P("row", col, None),
        P("row", col, None, None),
    )
    return jax.shard_map(
        on_device,
        mesh=grid,
        in_specs=placed,
        out_specs=P("row", col, None, None),
        check_vma=False,
    )
```

```python
import jax
import jax.numpy as jnp
from jax import lax
from jax.experimental import pallas as pl
from jax.experimental.pallas import tpu as pltpu
from jax.sharding import Mesh, PartitionSpec as P

W = 128
SLOTS = 64
HALF = 32
RBL = 32
CBL = 16
NZ = 16
ROWS = 16
ITERS = 2
PAD = 8
eps = 1e-06
SCALE = 0.25
TINY = 2.0**-64
LARGE = 1e37

F32 = jnp.float32
BF16 = jnp.bfloat16

SMEM = pl.BlockSpec(memory_space=pltpu.SMEM)
VMEM = pl.BlockSpec(memory_space=pltpu.VMEM)
PARAMS = pltpu.CompilerParams(vmem_limit_bytes=16 << 20)


def root(total):
    return jnp.sqrt(total + eps)


def halves(x):
    hi = x.astype(BF16)
    return hi, (x - hi.astype(F32)).astype(BF16)


def diagonal(count):
    shape = (count, W)
    return lax.broadcasted_iota(jnp.int32, shape, 0) == lax.broadcasted_iota(jnp.int32, shape, 1)


def to_row(col):
    return jnp.sum(jnp.where(diagonal(col.shape[0]), col, 0.0), axis=0, keepdims=True)


def to_col(row, count):
    return jnp.sum(jnp.where(diagonal(count), row, 0.0), axis=1, keepdims=True)


def spread(col):
    return jnp.broadcast_to(col, (col.shape[0], W))


def per_vector(squares):
    total = jnp.sum(squares, axis=1, keepdims=True)
    total = total[:HALF] + total[HALF:]
    return jnp.concatenate([total, total], axis=0)


def norm_rows(squares):
    return jnp.broadcast_to(to_row(per_vector(squares)), (PAD, W))


def add_product(slots, s, side, high, low, parts, acc, source, target, unused):
    both = jnp.concatenate([high, low], axis=1)
    prod = jnp.dot(parts[source(side, slots, s)], both, preferred_element_type=F32)
    prod = prod[:HALF, :W] + (prod[HALF:, :W] + prod[:HALF, W:])
    acc[jnp.where(slots[2, s] > 0, target(side, slots, s), unused)] += prod


def products(sides, parts, acc, source, target, unused):
    acc[...] = jnp.zeros_like(acc)
    for side, (slots, hi, lo) in enumerate(sides):
        for s in range(SLOTS):
            add_product(slots, s, side, hi[s], lo[s], parts, acc, source, target, unused)


def by_row(side, slots, s):
    return slots[0, s]


def by_col(side, slots, s):
    return slots[1, s] + side * CBL


def store_tiles(parts, first, second, x):
    hi, lo = halves(x * SCALE)
    parts[first] = jnp.concatenate([hi[:HALF], lo[:HALF]], axis=0)
    parts[second] = jnp.concatenate([hi[HALF:], lo[HALF:]], axis=0)


def emit_cols(out, acc, squares):
    norms = norm_rows(squares)
    for c in range(CBL):
        out[c, :HALF] = acc[c]
        out[c, HALF : 2 * HALF] = acc[CBL + c]
        out[c, 2 * HALF :] = norms


def first_products(slots, mats, kept, parts, acc):
    hi, lo, hi_t, lo_t = kept
    acc[...] = jnp.zeros_like(acc)
    for s in range(SLOTS):
        block = mats[s]
        high, low = halves(block)
        hi[s], lo[s] = high, low
        hi_t[s], lo_t[s] = halves(block.T)
        add_product(slots, s, 0, high, low, parts, acc, by_row, by_col, CBL)


def first_other_kernel(slots, mats, vec, hi, lo, hi_t, lo_t, parts, part, norms, acc):
    squares = jnp.zeros((2 * HALF, W), F32)
    for z in range(NZ):
        x = vec[z]
        squares += x * x
        store_tiles(parts, 2 * z, 2 * z + 1, x)
    norms[...] = norm_rows(squares)
    first_products(slots, mats, (hi, lo, hi_t, lo_t), parts, acc)
    part[...] = acc[:CBL]


def first_own_kernel(slots, mats, parts, part, norms, hi, lo, hi_t, lo_t, out, acc):
    first_products(slots, mats, (hi, lo, hi_t, lo_t), parts, acc)
    for c in range(CBL):
        out[c, :HALF] = acc[c]
        out[c, HALF : 2 * HALF] = part[c]
        out[c, 2 * HALF :] = norms[...]


def backward_kernel(slots0, slots1, hi0, lo0, hi1, lo1, vec, out, scale, factor, parts, acc):
    count = 2 * HALF
    total = jnp.zeros((PAD, W), F32)
    for z in range(NZ):
        total += vec[z, count:]
    alpha = root(to_col(total[:1], count))
    scale[...] = spread(alpha)
    inverse = spread(1.0 / (SCALE * alpha))
    factor[...] = inverse
    squares = jnp.zeros((count, W), F32)
    for z in range(NZ):
        x = vec[z, :count] * inverse
        squares += x * x
        store_tiles(parts, 2 * z, 2 * z + 1, x)
    sides = ((slots0, hi0, lo0), (slots1, hi1, lo1))
    products(sides, parts, acc, by_row, by_col, 2 * CBL)
    emit_cols(out, acc, squares)


def forward_kernel(slots0, slots1, hi0, lo0, hi1, lo1, vec, old, first, second, out, norms, parts, acc):
    count = 2 * HALF
    squares = jnp.zeros((count, W), F32)
    for c in range(CBL):
        x = vec[c]
        squares += x * x
        store_tiles(parts, c, CBL + c, x)
    sides = ((slots0, hi0, lo0), (slots1, hi1, lo1))
    products(sides, parts, acc, by_col, by_row, RBL)
    norms[...] = norm_rows(squares)
    weight = SCALE * spread(per_vector(squares))
    for z in range(NZ):
        less = weight * ((old[z, :count] * first[...]) * second[...])
        out[z, :HALF] = acc[2 * z] - less[:HALF]
        out[z, HALF:] = acc[2 * z + 1] - less[HALF:]


def summed(got):
    total = got[0]
    for index in range(1, got.shape[0]):
        total += got[index]
    return total


def first_cols_kernel(got, copies, fresh, scale, inverse):
    count = fresh.shape[0]
    total = summed(got)
    beta = root(to_col(total[count : count + 1], count))
    vec = total[:count] / (SCALE * beta)
    fresh[...] = vec
    copies[...] = jnp.broadcast_to(vec[None], copies.shape)
    scale[...] = spread(beta)
    inverse[...] = spread(1.0 / beta)


def cols_kernel(got, old, alpha, copies, fresh, scale, inverse):
    count = fresh.shape[0]
    total = summed(got)
    beta = root(to_col(total[count : count + 1], count))
    vec = total[:count] / (SCALE * beta) - beta * (old[...] / alpha[...])
    fresh[...] = vec
    copies[...] = jnp.broadcast_to(vec[None], copies.shape)
    scale[...] = spread(beta)
    inverse[...] = spread(1.0 / beta)


def rows_kernel(got, old, first, second, norms, fresh):
    count = first.shape[0]
    fresh[:count] = summed(got) - (SCALE * eps) * ((old[:count] * first[...]) * second[...])
    fresh[count:] = norms[...]


def lanes(start):
    shape = (2 * HALF, W)
    vector = lax.rem(lax.broadcasted_iota(jnp.int32, shape, 0), HALF)
    return lax.broadcasted_iota(jnp.int32, shape, 1) == vector + start


def row_at(squares, start):
    return jnp.sum(jnp.where(lanes(start), jnp.sum(squares, axis=1, keepdims=True), 0.0), axis=0, keepdims=True)


def col_at(row, start):
    return jnp.sum(jnp.where(lanes(start), row, 0.0), axis=1, keepdims=True)


def squares_kernel(piece, out):
    count = 2 * HALF
    vec = piece[:count]
    small = vec * TINY
    norms = col_at(piece[count : count + 1], 0) * (0.5 / ROWS)
    norms = jnp.sum(jnp.where(lanes(2 * HALF), norms, 0.0), axis=0, keepdims=True)
    out[...] = row_at(vec * vec, 0) + row_at(small * small, HALF) + norms


def last_kernel(got, scale_alpha, scale_beta):
    total = got[...]
    alpha = root(col_at(total, 2 * HALF))
    plain, small = col_at(total, 0), col_at(total, HALF)
    norm = jnp.where(plain < LARGE, jnp.sqrt(plain), jnp.sqrt(small) / TINY)
    norm = norm / (SCALE * alpha)
    scale_alpha[...] = spread(alpha)
    scale_beta[...] = spread(root(norm * norm))


def total_kernel(got, scale):
    scale[...] = spread(root(col_at(got[...], 0)))


def call(kernel, name, specs, outs, scratch=(), cost=None):
    return pl.pallas_call(
        kernel,
        out_shape=outs,
        in_specs=specs,
        out_specs=jax.tree.map(lambda _: VMEM, outs),
        scratch_shapes=scratch,
        compiler_params=PARAMS,
        cost_estimate=cost,
        name=name,
    )


def array(*shape):
    return jax.ShapeDtypeStruct(shape, F32)


def advance(state, vec, alpha, beta):
    x_vec, w_vec, phibar, rhobar = state
    rho = jnp.sqrt(rhobar * rhobar + beta * beta)
    cosine = rhobar / rho
    sine = beta / rho
    theta = sine * alpha
    rhobar = -cosine * alpha
    phi = cosine * phibar
    phibar = sine * phibar
    x_vec = x_vec + (phi / rho) * w_vec
    w_vec = vec - (theta / rho) * w_vec
    return (x_vec, w_vec, phibar, rhobar)


def on_device(blocks, block_rows, block_cols, block_valid, rhs):
    mats = blocks[0, 0]
    me = lax.axis_index("core")
    swap = [(0, 1), (1, 0)]
    count = 2 * HALF
    tile, rows_tile = array(count, W), array(PAD, W)
    copied, wide = array(CBL, count, W), array(CBL, count + PAD, W)
    halved = jax.ShapeDtypeStruct(mats.shape, BF16)

    def exchange(x, axis):
        return lax.all_to_all(x, axis, 0, 0, tiled=True)

    def other_core(x):
        return lax.ppermute(x, "core", swap)

    def in_order(mine, other):
        return jnp.concatenate([jnp.where(me == 0, mine, other), jnp.where(me == 0, other, mine)])

    def scratch(sources, targets):
        return (pltpu.VMEM((sources, 2 * HALF, W), BF16), pltpu.VMEM((targets + 1, HALF, W), F32))

    pieces = rhs[0, 0].reshape(2, HALF, W)
    mine = jnp.where(me == 0, pieces[0], pieces[1])
    rest = jnp.where(me == 0, pieces[1], pieces[0])
    mine, rest = lax.optimization_barrier((mine, rest))
    own_slots = jnp.stack([block_rows[0, 0], block_cols[0, 0], block_valid[0, 0]])
    listed = jnp.pad(own_slots.astype(F32), ((0, PAD - 3), (0, W - SLOTS)))
    got = other_core(jnp.concatenate([rest, listed]))
    slots = (own_slots, got[HALF : HALF + 3, :SLOTS].astype(jnp.int32))
    piece = in_order(mine, got[:HALF])
    other_mats, _ = lax.optimization_barrier((mats, got))
    other_mats = other_core(other_mats)
    specs = [SMEM] * 2 + [VMEM] * 5

    def first_backward():
        full = lax.all_gather(piece, "z")
        parts = jax.ShapeDtypeStruct((RBL, 2 * HALF, W), BF16)
        acc = (pltpu.VMEM((CBL + 1, HALF, W), F32),)
        outs = (halved,) * 4 + (parts, array(CBL, HALF, W), rows_tile)
        cost = pl.CostEstimate(flops=SLOTS * 2**22, bytes_accessed=SLOTS * 3 * 2**16, transcendentals=0)
        apply = call(first_other_kernel, "apply_first_other", [SMEM] + [VMEM] * 2, outs, acc, cost)
        *kept1, parts, part, norms = apply(slots[1], other_mats, full)
        outs = (halved,) * 4 + (wide,)
        apply = call(first_own_kernel, "apply_first_own", [SMEM] + [VMEM] * 4, outs, acc, cost)
        *kept0, out = apply(slots[0], mats, parts, part, norms)
        return exchange(out, "row"), full, (*kept0[:2], *kept1[:2]), (*kept0[2:], *kept1[2:])

    def backward(fresh):
        full = lax.all_gather(fresh, "z")
        apply = call(backward_kernel, "apply_transposed", specs, (wide, tile, tile), scratch(RBL, 2 * CBL))
        part, alpha, factor = apply(*slots, *plain, full)
        return exchange(part, "row"), full, alpha, factor

    def forward(copies, full, first, second):
        vec = exchange(copies, "row")
        apply = call(
            forward_kernel, "apply_plain", specs + [VMEM] * 3, (copied, rows_tile), scratch(2 * CBL, RBL)
        )
        part, norms = apply(*slots, *turned, vec, full, first, second)
        return exchange(part, "z"), norms

    def everywhere(row):
        copies = jnp.broadcast_to(row[None], (ROWS * NZ, 1, W))
        return jnp.sum(exchange(copies, ("row", "z")), axis=0)

    got, full, plain, turned = first_backward()
    outs = (copied, tile, tile, tile)
    copies, v_old, beta, second = call(first_cols_kernel, "first_cols", [VMEM], outs)(got)
    u_old, first = piece, jnp.ones((count, W), F32)
    state = None
    for step_index in range(ITERS):
        got, norms = forward(copies, full, first, second)
        fresh = call(rows_kernel, "rows", [VMEM] * 5, array(count + PAD, W))(got, u_old, first, second, norms)
        got, full, alpha, first = backward(fresh)
        u_old = fresh
        if step_index == ITERS - 1:
            last = everywhere(call(squares_kernel, "squares", [VMEM], array(1, W))(fresh))
            alpha, last_beta = call(last_kernel, "last", [VMEM], (tile, tile))(last)
        v_now = v_old / alpha
        if state is None:
            state = (jnp.zeros_like(v_now), v_now, beta, alpha)
        else:
            state = advance(state, v_now, alpha, beta)
        copies, v_old, beta, second = call(cols_kernel, "cols", [VMEM] * 3, outs)(got, v_old, alpha)
    squares = jnp.sum(v_old * v_old, axis=1)
    squares = squares[:HALF] + squares[HALF:]
    total = everywhere(jnp.pad(squares, (0, W - HALF))[None])
    alpha = call(total_kernel, "total", [VMEM], tile)(total)
    x_vec = advance(state, v_old / alpha, alpha, last_beta)[0]
    return in_order(x_vec[:HALF], other_core(x_vec[HALF:]))[None, None]


def solution(mesh):
    grid = Mesh(mesh.devices.reshape(16, NZ, 2), ("row", "z", "core"))
    col = ("z", "core")
    placed = (
        P("row", col, None, None, None),
        P("row", col, None),
        P("row", col, None),
        P("row", col, None),
        P("row", col, None, None),
    )
    return jax.shard_map(
        on_device,
        mesh=grid,
        in_specs=placed,
        out_specs=P("row", col, None, None),
        check_vma=False,
    )
```
